256 devices in a mesh: span: 32 (over y, x, core), chord: 8 (over z).
Axes of the slice: x: 4, y: 4, z: 8, core: 2. Of those that a mesh axis runs over, the one named last changes fastest.
Arguments:
- right_side: float32 [162, 32768], P(None, ('span', 'chord')), may hold values from -8 to 8
- diag_blocks: bfloat16 [162, 162, 32768], P(None, None, ('span', 'chord')), may hold values from -0.25 to 3.1
- face_blocks: bfloat16 [6, 54, 54, 32768], P(None, None, None, ('span', 'chord')), may hold values from -0.29882812 to 0.29882812
- orient_codes: int32 [6, 32768], P(None, ('span', 'chord')), may hold values from 0 to 7
- live_counts: int32 [256], P(('span', 'chord')), may hold values from 1 to 128, 24576 in all
- shifts: float32 [4], replicated, may hold values from 0.8 to 2.5
- shift_order: int32 [4], replicated, may hold values from 0 to 3, each once
Outputs:
- adjoint: float32 [162, 32768], P(None, ('span', 'chord'))
- residual: float32 [162, 32768], P(None, ('span', 'chord'))
- coefficients: float32 [3, 4], replicated
The draws below stay inside these ranges and needn't reach their ends.
Inputs may be any that keep to these rules, and one draw needn't show every extreme that they name: `live_counts`: each partition holds at least one live element, and some partition holds 128. `shift_order`: each value once.
All inputs are finite; a program needn't handle non-finite values. No bound on the sum of `live_counts` on one device may be relied on, other than what follows from the above.
Results may differ from the reference program's by a relative error of at most 0.0012.
Values sent between devices are 32-bit elements; how exact they have to be, the bound alone decides.
A program may use at most 128 MiB of HBM per device.

```python
import math
import jax
import jax.numpy as jnp
import numpy as np
from jax import lax

BLOCK = 162
FACE = 54
E_DEV = 128
S_STEPS = 4
CYCLES = 3
ELEMS = 32768
N_SPAN = 32
N_CHORD = 8


def draw_diag_blocks(key, part):
    key = jax.random.fold_in(key, 11)
    first_key, second_key = jax.random.split(key)
    spread = jnp.clip(jax.random.normal(first_key, (BLOCK, BLOCK, ELEMS), jnp.float32), -4.0, 4.0) * (0.4 / BLOCK ** 0.5)
    middle = jax.random.uniform(second_key, (BLOCK, ELEMS), jnp.float32, 1.0, 2.5)
    identity = jnp.eye(BLOCK, dtype=jnp.float32)
    return (spread + identity[:, :, None] * middle[None, :, :]).astype(jnp.bfloat16)


def plant(values, rng, least, largest):
    longest = values.shape.index(max(values.shape))
    spots = []
    for shift in (0, 1):
        where = [jax.random.randint(jax.random.fold_in(rng, axis), (), 0, length) for axis, length in enumerate(values.shape)]
        where[longest] = (where[longest] + shift) % values.shape[longest]
        spots.append(tuple(where))
    return values.at[spots[0]].set(least).at[spots[1]].set(largest)


def shard_levels(rng, extent, cuts, low, top_value):
    loudness, own = 1.0, jax.random.fold_in(rng, 6)
    for position, shards_of in cuts:
        steps = jnp.exp(jax.random.uniform(jax.random.fold_in(own, position), (shards_of,), jnp.float32, low / len(cuts), top_value / len(cuts)))
        loudness = loudness * jnp.repeat(steps, extent[position] // shards_of).reshape([-1 if axis == position else 1 for axis in range(len(extent))])
    return loudness


def split_up(number_of, total, reach, slope):
    loads = [(1 << 20) // math.isqrt(grade ** slope) + 1 for grade in range(2, number_of + 1)]
    rest, holding = total - reach - (number_of - 1), [1] * (number_of - 1)
    while rest > 0:
        candidates = [i for i in range(number_of - 1) if holding[i] < reach]
        mass, left = sum([loads[i] for i in candidates]), rest
        for i in candidates:
            more = min(reach - holding[i], max(1, left * loads[i] // mass), rest)
            holding[i] = holding[i] + more
            rest = rest - more
    return np.array([reach] + holding)


def uneven_parts(own_key, number_of, total, most, slope):
    if number_of == 2:
        one = jax.random.randint(own_key, (), max(1, total - most), min(most, total - 1) + 1)
        return jnp.stack([one, total - one])
    sizes = jnp.asarray(split_up(number_of, total, most, slope), jnp.int32)
    pairs = (number_of - 1) // 2
    source_of, taker = sizes[1:1 + 2 * pairs:2], sizes[2:2 + 2 * pairs:2]
    room = jnp.minimum(source_of - 1, most - taker)
    shifted = jax.random.randint(jax.random.fold_in(own_key, 1), (pairs,), 0, 1 << 20) % (room + 1)
    sizes = sizes.at[1:1 + 2 * pairs:2].set(source_of - shifted).at[2:2 + 2 * pairs:2].set(taker + shifted)
    return sizes[jax.random.permutation(jax.random.fold_in(own_key, 2), number_of)]


def bell_draw(stream_key, dims, scale, reach, cuts=(), held_as=jnp.bfloat16):
    drawn = scale * jax.random.normal(stream_key, dims, jnp.float32)
    if cuts:
        drawn = drawn * shard_levels(stream_key, dims, cuts, -0.22, 0.18)
    return jnp.clip(drawn, -reach, reach).astype(held_as)


def setup_inputs(seed: int = 0) -> dict:
    splits = jax.random.split(jax.random.key(seed), 8)
    return {
        "right_side": bell_draw(splits[0], (BLOCK, ELEMS), 1.0, 8.0, ((1, 256),), jnp.float32),
        "diag_blocks": draw_diag_blocks(jax.random.fold_in(splits[7], 71), 0),
        "face_blocks": bell_draw(splits[2], (6, FACE, FACE, ELEMS), 0.05, 0.29882812, ((3, 256),)),
        "orient_codes": plant(jax.random.randint(splits[3], (6, ELEMS), 0, 8), jax.random.fold_in(splits[3], 1), 0, 7).astype(jnp.int32),
        "live_counts": uneven_parts(splits[4], N_SPAN * N_CHORD, N_SPAN * N_CHORD * E_DEV * 3 // 4, E_DEV, 2).astype(jnp.int32),
        "shifts": jnp.clip(jnp.exp(jax.random.uniform(splits[5], (S_STEPS,), jnp.float32, math.log(0.8), math.log(2.5))), 0.8, 2.5),
        "shift_order": jax.random.permutation(splits[6], S_STEPS).astype(jnp.int32),
    }


face_spots = ((1, 0), (1, 2), (2, 0), (2, 2), (3, 0), (3, 2))

def orient_faces(face_values, face_codes):
    result = jnp.zeros_like(face_values)
    for pattern in range(8):
        variant = face_values
        if pattern & 4:
            variant = jnp.swapaxes(variant, 1, 2)
        if pattern & 1:
            variant = jnp.flip(variant, 1)
        if pattern & 2:
            variant = jnp.flip(variant, 2)
        result = result + jnp.where(face_codes == pattern, variant, 0.0)
    return result

def block_product(blocks, vector):
    groups = vector.shape[-1] // E_DEV

    def one_group(start):
        block_piece = lax.dynamic_slice_in_dim(blocks, start, E_DEV, 2).astype(jnp.float32)
        column = lax.dynamic_slice_in_dim(vector, start, E_DEV, 1)
        return jnp.einsum('pqn,pn->qn', block_piece, column, precision=lax.Precision.HIGHEST)
    starts = (jnp.arange(groups) * E_DEV).astype(jnp.int32)
    pieces = lax.map(one_group, starts)
    return jnp.moveaxis(pieces, 0, 1).reshape(blocks.shape[1], vector.shape[-1])

def slide(values, axis_pos, offset):
    length = values.shape[axis_pos]
    zero_layer = jnp.zeros_like(lax.slice_in_dim(values, 0, 1, axis=axis_pos))
    if offset > 0:
        return jnp.concatenate([zero_layer, lax.slice_in_dim(values, 0, length - 1, axis=axis_pos)], axis=axis_pos)
    return jnp.concatenate([lax.slice_in_dim(values, 1, length, axis=axis_pos), zero_layer], axis=axis_pos)

def place_face(nodal_values, arriving, axis_pos, node_spot):
    if axis_pos == 1:
        return nodal_values.at[:, node_spot].add(arriving)
    if axis_pos == 2:
        return nodal_values.at[:, :, node_spot].add(arriving)
    return nodal_values.at[:, :, :, node_spot].add(arriving)

def apply_transposed(vector, diag_blocks, face_blocks, orient_codes, alive_mask):
    elements = vector.shape[-1]
    nodal_values = vector.reshape(-1, 3, 3, 3, elements)
    result = block_product(diag_blocks, vector).reshape(nodal_values.shape)
    partials = []
    for face_index in range(6):
        axis_pos, node_spot = face_spots[face_index]
        trace_part = lax.index_in_dim(nodal_values, node_spot, axis_pos, keepdims=False)
        product = block_product(face_blocks[face_index], trace_part.reshape(-1, elements))
        partials.append(orient_faces(product.reshape(trace_part.shape), orient_codes[face_index]))
    face_shape = partials[0].shape
    grid_shape = face_shape[:3] + (N_SPAN, N_CHORD, E_DEV)
    grids = [part_value.reshape(grid_shape) for part_value in partials]
    arriving = [slide(grids[1], 3, 1), slide(grids[0], 3, -1), slide(grids[3], 4, 1), slide(grids[2], 4, -1), slide(grids[5], 5, 1), slide(grids[4], 5, -1)]
    for face_index in range(6):
        axis_pos, node_spot = face_spots[face_index]
        result = place_face(result, arriving[face_index].reshape(face_shape), axis_pos, node_spot)
    return jnp.where(alive_mask, result.reshape(-1, elements), 0.0)

def reference(right_side, diag_blocks, face_blocks, orient_codes, live_counts, shifts, shift_order):
    highest = lax.Precision.HIGHEST
    elements = right_side.shape[-1]
    slot_index = jnp.arange(elements, dtype=jnp.int32) % E_DEV
    owner_index = jnp.arange(elements, dtype=jnp.int32) // E_DEV
    alive_mask = slot_index < live_counts[owner_index]
    thetas = shifts[shift_order]
    bidiagonal = jnp.concatenate([jnp.diag(thetas), jnp.zeros((1, S_STEPS), jnp.float32)], 0)
    bidiagonal = bidiagonal + jnp.eye(S_STEPS + 1, S_STEPS, -1, dtype=jnp.float32)
    residual = jnp.where(alive_mask, right_side, 0.0)
    adjoint = jnp.zeros_like(residual)
    coefficients = []
    for cycle_index in range(CYCLES):
        krylov_basis = [residual]
        for step_index in range(S_STEPS):
            current = krylov_basis[step_index]
            image = apply_transposed(current, diag_blocks, face_blocks, orient_codes, alive_mask)
            krylov_basis.append(image - thetas[step_index] * current)
        flattened = jnp.stack(krylov_basis).reshape(S_STEPS + 1, -1)
        gram_matrix = jnp.dot(flattened, flattened.T, precision=highest)
        normal_matrix = jnp.dot(jnp.dot(bidiagonal.T, gram_matrix, precision=highest), bidiagonal, precision=highest)
        target = jnp.dot(bidiagonal.T, gram_matrix[:, 0], precision=highest)
        factor = jnp.linalg.cholesky(normal_matrix)
        weights = jax.scipy.linalg.cho_solve((factor, True), target)
        combined = jnp.dot(bidiagonal, weights, precision=highest)
        for step_index in range(S_STEPS):
            adjoint = adjoint + weights[step_index] * krylov_basis[step_index]
        for step_index in range(S_STEPS + 1):
            residual = residual - combined[step_index] * krylov_basis[step_index]
        coefficients.append(weights)
    return (adjoint, residual, jnp.stack(coefficients))
```

```python
import functools

import jax
import jax.numpy as jnp
from jax import lax
from jax.experimental import pallas as pl
from jax.experimental.pallas import tpu as pltpu
from jax.sharding import PartitionSpec as P

MESH = pl.DeviceIdType.MESH
F32 = jnp.float32

CYCLES = 3
STEPS = 4
AHEAD = 2
TOTAL = 12
BLOCK = 162
FACE = 54
NVAR = 6
ROWS = 168
ELEMS = 128
SPANS = 32
CHORDS = 8
GROUP = 16
ENTRIES = 15
CHUNK = 18
SPOTS = ((1, 0), (1, 2), (2, 0), (2, 2), (3, 0), (3, 2))


def node_of(face, s, t):
    axis_pos, spot = SPOTS[face]
    place = [s, t]
    place.insert(axis_pos - 1, spot)
    return place[0] * 9 + place[1] * 3 + place[2]


def pair_index(i, j):
    i, j = min(i, j), max(i, j)
    return i * 5 - i * (i - 1) // 2 + (j - i)


def kernel(
    rhs_hbm, diag_hbm, face_hbm, codes, live, shifts, order,
    adj_out, res_out, coef_out,
    dstage, fstage, diag, face, basis, adj, prod, result, local, sbuf, rbuf, gacc, slots,
    rhs_sem, dsem, fsem, send_sem, recv_sem, gsend_sem, grecv_sem,
):
    span, chord = lax.axis_index("span"), lax.axis_index("chord")
    core, chip = lax.rem(span, 2), span // 2

    rhs_copy = pltpu.make_async_copy(rhs_hbm, basis.at[0, pl.ds(0, BLOCK)], rhs_sem)
    rhs_copy.start()
    face_copies = {
        g: pltpu.make_async_copy(face_hbm.at[g], fstage.at[g], fsem.at[g]) for g in range(6)
    }
    for g in (2, 3, 0, 1, 4, 5):
        face_copies[g].start()

    def diag_copy(i):
        rows = pl.ds(i * CHUNK, CHUNK)
        return pltpu.make_async_copy(diag_hbm.at[rows], dstage.at[rows], dsem.at[i])

    for i in range(BLOCK // CHUNK):
        diag_copy(i).start()

    neighbours = (
        (lax.rem(span + SPANS - 1, SPANS), chord),
        (lax.rem(span + 1, SPANS), chord),
        (span, lax.rem(chord + CHORDS - 1, CHORDS)),
        (span, lax.rem(chord + 1, CHORDS)),
    )
    me_in = (chord * 2 + core, chip)

    def partner(phase, off):
        there = lax.rem(me_in[phase] + off, GROUP)
        if phase == 0:
            return (chip * 2 + lax.rem(there, 2), there // 2)
        return (there * 2 + core, chord)

    barrier = pltpu.get_barrier_semaphore()
    for to in neighbours[:2]:
        pl.semaphore_signal(barrier, inc=1, device_id=to, device_id_type=MESH)
    for phase in range(2):
        for off in range(1, GROUP):
            pl.semaphore_signal(
                barrier, inc=1, device_id=partner(phase, off), device_id_type=MESH
            )

    alive = lax.broadcasted_iota(jnp.int32, (8, ELEMS), 1) < live[0]
    alive6 = alive[:NVAR]
    lane6 = lax.broadcasted_iota(jnp.int32, (NVAR, ELEMS), 1)
    eye = lax.broadcasted_iota(jnp.int32, (GROUP, ELEMS), 0) == lax.broadcasted_iota(
        jnp.int32, (GROUP, ELEMS), 1
    )
    thetas = [shifts[order[k]] for k in range(STEPS)]
    keep = (
        (span > 0).astype(F32),
        (span < SPANS - 1).astype(F32),
        (chord > 0).astype(F32),
        (chord < CHORDS - 1).astype(F32),
    )

    for k in range(1, STEPS + AHEAD + 1):
        basis[k, pl.ds(160, 8), :] = jnp.zeros((8, ELEMS), F32)
    adj[...] = jnp.zeros_like(adj)
    gacc[...] = jnp.zeros_like(gacc)
    rhs_copy.wait()
    for i in range(0, 160, 8):
        basis[0, pl.ds(i, 8), :] = jnp.where(alive, basis[0, pl.ds(i, 8), :], 0.0)
    tail = jnp.where(alive[:2], basis[0, pl.ds(160, 2), :], 0.0)
    basis[0, pl.ds(160, 8), :] = jnp.zeros((8, ELEMS), F32)
    basis[0, pl.ds(160, 2), :] = tail

    def remote(step, g):
        return pltpu.make_async_remote_copy(
            src_ref=sbuf.at[step, g],
            dst_ref=rbuf.at[step, g ^ 1],
            send_sem=send_sem.at[step, g],
            recv_sem=recv_sem.at[step, g ^ 1],
            device_id=neighbours[g],
            device_id_type=MESH,
        )

    def face_products(k, faces, first):
        def some(v, sums):
            sums = list(sums)
            for j in range(9):
                for n, g in enumerate(faces):
                    if first:
                        block = fstage[g, v * 9 + j].astype(F32)
                        face[g, v * 9 + j] = block
                    else:
                        block = face[g, v * 9 + j]
                    row = v * 27 + node_of(g, j // 3, j % 3)
                    sums[n] = sums[n] + block * basis[k, pl.ds(row, 1), :]
            return tuple(sums)

        def body(i, sums):
            for u in range(3):
                sums = some(i * 3 + u, sums)
            return sums

        zero = tuple(jnp.zeros((FACE, ELEMS), F32) for _ in faces)
        return lax.fori_loop(0, NVAR // 3, body, zero)

    def oriented(g, product):
        prod[g, pl.ds(0, FACE), :] = product
        y = [[prod[g, pl.ds(3 * s + t, NVAR, stride=9), :] for t in range(3)] for s in range(3)]
        code = jnp.broadcast_to(codes[pl.ds(g, 1), :], (NVAR, ELEMS))
        swap, flip_s, flip_t = [(code & bit) != 0 for bit in (4, 1, 2)]
        y = [[y[s][t] if s == t else jnp.where(swap, y[t][s], y[s][t]) for t in range(3)] for s in range(3)]
        y = [[y[s][t] if s == 1 else jnp.where(flip_s, y[2 - s][t], y[s][t]) for t in range(3)] for s in range(3)]
        return [[y[s][t] if t == 1 else jnp.where(flip_t, y[s][2 - t], y[s][t]) for t in range(3)] for s in range(3)]

    def do_faces(step, k, faces, first):
        products = face_products(k, faces, first)
        for g, product in zip(faces, products):
            y = oriented(g, product)
            for s in range(3):
                for t in range(3):
                    if g < 4:
                        sbuf[step, g, pl.ds(3 * s + t, NVAR, stride=9), :] = y[s][t]
                    elif g == 5:
                        moved = pltpu.roll(y[s][t], 1, 1)
                        local[0, 3 * s + t] = jnp.where(lane6 == 0, 0.0, moved)
                    else:
                        moved = pltpu.roll(y[s][t], ELEMS - 1, 1)
                        local[1, 3 * s + t] = jnp.where(lane6 == ELEMS - 1, 0.0, moved)
            if g < 4:
                remote(step, g).start()

    def diag_product(k, first):
        def body(i, total):
            if first:
                diag_copy(i).wait()
            for u in range(CHUNK):
                p = i * CHUNK + u
                if first:
                    block = dstage[p].astype(F32)
                    diag[p] = block
                else:
                    block = diag[p]
                total = total + block * basis[k, pl.ds(p, 1), :]
            return total

        result[...] = lax.fori_loop(0, BLOCK // CHUNK, body, jnp.zeros((BLOCK, ELEMS), F32))

    def finish_product(step, k, theta):
        for g in range(4):
            remote(step, g).wait_recv()
        for a in range(3):
            for b in range(3):
                for c in range(3):
                    rows = pl.ds(9 * a + 3 * b + c, NVAR, stride=27)
                    value = result[rows, :]
                    for at, g, (s, t) in ((a, 0, (b, c)), (b, 2, (a, c))):
                        if at != 1:
                            side = g + at // 2
                            got = rbuf[step, side, pl.ds(3 * s + t, NVAR, stride=9), :]
                            value = value + got * keep[side]
                    if c != 1:
                        value = value + local[c // 2, 3 * a + b]
                    value = jnp.where(alive6, value, 0.0)
                    basis[k + 1, rows, :] = value - theta * basis[k, rows, :]
        for g in range(4):
            remote(step, g).wait_send()

    def product(step, k, theta, first):
        for pair in ((2, 3), (0, 1), (4, 5)):
            if first:
                for g in pair:
                    face_copies[g].wait()
                if pair == (2, 3):
                    pl.semaphore_wait(barrier, 2 * GROUP)
            do_faces(step, k, pair, first)
        diag_product(k, first)
        finish_product(step, k, theta)

    def phase_copy(cycle, phase, off, count=None):
        place = pl.ds(0, count) if count else me_in[phase]
        ref = slots.at[cycle, phase, place]
        return pltpu.make_async_remote_copy(
            src_ref=ref,
            dst_ref=ref,
            send_sem=gsend_sem.at[cycle, phase],
            recv_sem=grecv_sem.at[cycle, phase],
            device_id=partner(phase, off),
            device_id_type=MESH,
        )

    def send_phase(cycle, phase, row):
        slots[cycle, phase, me_in[phase]] = row
        for off in range(1, GROUP):
            phase_copy(cycle, phase, off).start()

    def take_phase(cycle, phase):
        copy = phase_copy(cycle, phase, 1, GROUP - 1)
        copy.wait_send()
        copy.wait_recv()
        return jnp.sum(slots[cycle, phase], axis=0)

    def start_gram(cycle):
        def body(i, sums):
            sums = list(sums)
            for u in range(3):
                v = [basis[k, pl.ds(pl.multiple_of(i * 24 + u * 8, 8), 8), :] for k in range(5)]
                for a in range(5):
                    for b in range(a, 5):
                        e = pair_index(a, b)
                        sums[e] = sums[e] + v[a] * v[b]
            return tuple(sums)

        sums = lax.fori_loop(
            0, ROWS // 24, body, tuple(jnp.zeros((8, ELEMS), F32) for _ in range(ENTRIES))
        )
        for e in range(ENTRIES):
            gacc[pl.ds(8 * e, 8), :] = sums[e]
        part = gacc[pl.ds(0, GROUP, stride=8), :]
        for r in range(1, 8):
            part = part + gacc[pl.ds(r, GROUP, stride=8), :]
        column = jnp.sum(part, axis=1, keepdims=True)
        row = jnp.sum(jnp.where(eye, column, 0.0), axis=0, keepdims=True)
        send_phase(cycle, 0, row)

    def middle_gram(cycle):
        send_phase(cycle, 1, take_phase(cycle, 0))

    def end_gram(cycle):
        row = take_phase(cycle, 1)
        spread = jnp.sum(jnp.where(eye, row, 0.0), axis=1, keepdims=True)
        spread = jnp.broadcast_to(spread, (GROUP, ELEMS))
        gram = [
            [spread[pair_index(i, j):pair_index(i, j) + 1] for j in range(5)] for i in range(5)
        ]
        half = [[gram[i][k] * thetas[k] + gram[i][k + 1] for k in range(4)] for i in range(5)]
        normal = [[half[j][k] * thetas[j] + half[j + 1][k] for k in range(4)] for j in range(4)]
        target = [gram[j][0] * thetas[j] + gram[j + 1][0] for j in range(4)]
        low = [[None] * 4 for _ in range(4)]
        scaled = [[None] * 4 for _ in range(4)]
        inverse = [None] * 4
        for j in range(4):
            for i in range(j, 4):
                value = normal[i][j]
                for m in range(j):
                    value = value - low[j][m] * scaled[i][m]
                scaled[i][j] = value
            inverse[j] = 1.0 / scaled[j][j]
            for i in range(j + 1, 4):
                low[i][j] = scaled[i][j] * inverse[j]
        fore = []
        for i in range(4):
            value = target[i]
            for m in range(i):
                value = value - low[i][m] * fore[m]
            fore.append(value)
        weights = [None] * 4
        for i in reversed(range(4)):
            value = fore[i] * inverse[i]
            for m in range(i + 1, 4):
                value = value - low[m][i] * weights[m]
            weights[i] = value
        combined = [weights[0] * thetas[0]]
        for i in range(1, 4):
            combined.append(weights[i] * thetas[i] + weights[i - 1])
        combined.append(weights[3])
        lanes = lax.broadcasted_iota(jnp.int32, (1, ELEMS), 1)
        line = jnp.zeros((1, ELEMS), F32)
        for i in range(4):
            line = jnp.where(lanes == i, weights[i], line)
        coef_out[pl.ds(cycle, 1), :] = line[:, :STEPS]
        return weights, combined

    def wide(values):
        return [jnp.broadcast_to(value, (8, ELEMS)) for value in values]

    def next_cycle(cycle):
        weights, combined = end_gram(cycle)
        weights8, combined8 = wide(weights), wide(combined)
        sets = [[1.0 - combined[0]] + [-value for value in combined[1:]]]
        for m in range(AHEAD):
            old = sets[-1]
            new = [None] * (len(old) + 1)
            for i, value in enumerate(old):
                here = value * (thetas[i % STEPS] - thetas[m])
                new[i] = here if new[i] is None else new[i] + here
                new[i + 1] = value
            sets.append(new)
        sets8 = [wide(one) for one in sets]

        def body(i, carry):
            rows = pl.ds(pl.multiple_of(i * 8, 8), 8)
            v = [basis[k, rows, :] for k in range(STEPS + AHEAD + 1)]
            total = adj[rows, :]
            for k in range(STEPS):
                total = total + weights8[k] * v[k]
            adj[rows, :] = total
            fresh = v[0]
            for k in range(STEPS + 1):
                fresh = fresh - combined8[k] * v[k]
            basis[0, rows, :] = fresh
            for m in range(1, AHEAD + 1):
                total = sets8[m][0] * v[0]
                for k in range(1, len(sets8[m])):
                    total = total + sets8[m][k] * v[k]
                basis[m, rows, :] = total
            return carry

        lax.fori_loop(0, ROWS // 8, body, 0)

    def last_cycle(cycle):
        weights, combined = end_gram(cycle)
        weights8, combined8 = wide(weights), wide(combined)
        for i in range(0, BLOCK, 8):
            size = min(8, BLOCK - i)
            rows = pl.ds(i, size)
            v = [basis[k, rows, :] for k in range(STEPS + 1)]
            total = adj[rows, :]
            for k in range(STEPS):
                total = total + weights8[k][:size] * v[k]
            adj_out[rows, :] = total
            fresh = v[0]
            for k in range(STEPS + 1):
                fresh = fresh - combined8[k][:size] * v[k]
            res_out[rows, :] = fresh

    product(0, 0, thetas[0], True)

    def step_body(step, carry):
        k = jnp.where(step < 2, step, lax.rem(step + 2, 4) + 2)
        product(step, k, shifts[order[lax.rem(k, STEPS)]], False)
        place = lax.rem(step, 4)
        cycle = step // 4

        @pl.when(place == 3)
        def _():
            start_gram(cycle)

        @pl.when(jnp.logical_and(place == 0, step >= 4))
        def _():
            middle_gram(cycle - 1)

        @pl.when(jnp.logical_and(place == 1, step >= 4))
        def _():
            next_cycle(cycle - 1)

        return carry

    lax.fori_loop(1, TOTAL, step_body, 0)
    middle_gram(CYCLES - 1)
    last_cycle(CYCLES - 1)


def on_device(right_side, diag_blocks, face_blocks, orient_codes, live_counts, shifts, shift_order):
    vmem = pl.BlockSpec(memory_space=pltpu.VMEM)
    smem = pl.BlockSpec(memory_space=pltpu.SMEM)
    anywhere = pl.BlockSpec(memory_space=pl.ANY)
    return pl.pallas_call(
        kernel,
        out_shape=(
            jax.ShapeDtypeStruct((BLOCK, ELEMS), F32),
            jax.ShapeDtypeStruct((BLOCK, ELEMS), F32),
            jax.ShapeDtypeStruct((CYCLES, STEPS), F32),
        ),
        in_specs=[anywhere, anywhere, anywhere, vmem, smem, smem, smem],
        out_specs=(vmem, vmem, vmem),
        scratch_shapes=[
            pltpu.VMEM((BLOCK, BLOCK, ELEMS), jnp.bfloat16),
            pltpu.VMEM((6, FACE, FACE, ELEMS), jnp.bfloat16),
            pltpu.VMEM((BLOCK, BLOCK, ELEMS), F32),
            pltpu.VMEM((6, FACE, FACE, ELEMS), F32),
            pltpu.VMEM((STEPS + AHEAD + 1, ROWS, ELEMS), F32),
            pltpu.VMEM((ROWS, ELEMS), F32),
            pltpu.VMEM((6, 56, ELEMS), F32),
            pltpu.VMEM((BLOCK, ELEMS), F32),
            pltpu.VMEM((2, 9, NVAR, ELEMS), F32),
            pltpu.VMEM((TOTAL, 4, FACE, ELEMS), F32),
            pltpu.VMEM((TOTAL, 4, FACE, ELEMS), F32),
            pltpu.VMEM((GROUP * 8, ELEMS), F32),
            pltpu.VMEM((CYCLES, 2, GROUP, 1, ELEMS), F32),
            pltpu.SemaphoreType.DMA,
            pltpu.SemaphoreType.DMA((BLOCK // CHUNK,)),
            pltpu.SemaphoreType.DMA((6,)),
            pltpu.SemaphoreType.DMA((TOTAL, 4)),
            pltpu.SemaphoreType.DMA((TOTAL, 4)),
            pltpu.SemaphoreType.DMA((CYCLES, 2)),
            pltpu.SemaphoreType.DMA((CYCLES, 2)),
        ],
        compiler_params=pltpu.CompilerParams(
            collective_id=0, has_side_effects=True, vmem_limit_bytes=56 * 2**20
        ),
    )(right_side, diag_blocks, face_blocks, orient_codes, live_counts, shifts, shift_order)


def solution(mesh):
    placed = (
        P(None, ("span", "chord")),
        P(None, None, ("span", "chord")),
        P(None, None, None, ("span", "chord")),
        P(None, ("span", "chord")),
        P(("span", "chord")),
        P(),
        P(),
    )
    return jax.shard_map(
        on_device,
        mesh=mesh,
        in_specs=placed,
        out_specs=(P(None, ("span", "chord")), P(None, ("span", "chord")), P()),
        check_vma=False,
    )
```

```python
import functools

import jax
import jax.numpy as jnp
from jax import lax
from jax.experimental import pallas as pl
from jax.experimental.pallas import tpu as pltpu
from jax.sharding import PartitionSpec as P

MESH = pl.DeviceIdType.MESH
F32 = jnp.float32

CYCLES = 3
STEPS = 4
AHEAD = 4
TOTAL = 12
BLOCK = 162
FACE = 54
NVAR = 6
NODES = 27
ELEMS = 128
SPANS = 32
CHORDS = 8
GROUP = 16
ENTRIES = 15
CHUNK = 27

def node_of(axis, side, j):
    if axis == 0:
        return side * 18 + j
    if axis == 1:
        return (j // 3) * 9 + side * 6 + j % 3
    return j * 3 + side * 2


def pair_index(i, j):
    i, j = min(i, j), max(i, j)
    return i * 5 - i * (i - 1) // 2 + (j - i)


def kernel(
    rhs_hbm, diag_hbm, face_hbm, codes_hbm, live_hbm, shifts_hbm, order_hbm,
    adj_out, res_out, coef_out,
    dstage, fstage, diag, face, rhs, codes, live, shifts, order, basis, adj, prod, result, local, masks, sbuf, rbuf,
    gacc, slots,
    small_sem, dsem, fsem, send_sem, recv_sem, gsend_sem, grecv_sem,
):
    span, chord = lax.axis_index("span"), lax.axis_index("chord")
    core, chip = lax.rem(span, 2), span // 2
    inner = (chord < CHORDS // 2).astype(jnp.int32)
    far, middle, outer, near = (0, core), (1, inner), (1, 1 - inner), (0, 1 - core)

    small_copies = [
        pltpu.make_async_copy(source, target, small_sem.at[i])
        for i, (source, target) in enumerate(
            (
                (rhs_hbm, rhs),
                (live_hbm, live),
                (codes_hbm, codes),
                (shifts_hbm, shifts),
                (order_hbm, order),
            )
        )
    ]
    for copy in small_copies[:2]:
        copy.start()

    def face_copy(axis, side):
        g = 2 * axis + side
        return pltpu.make_async_copy(face_hbm.at[g], fstage.at[g], fsem.at[g])

    face_copy(*far).start()
    for copy in small_copies[2:]:
        copy.start()
    for one in (middle, outer, near, (2, 0), (2, 1)):
        face_copy(*one).start()

    def diag_copy(i):
        rows = pl.ds(i * CHUNK, CHUNK)
        return pltpu.make_async_copy(diag_hbm.at[rows], dstage.at[rows], dsem.at[i])

    for i in range(BLOCK // CHUNK):
        diag_copy(i).start()

    def neighbour(axis, side):
        if axis == 0:
            return (lax.rem(span + SPANS + 2 * side - 1, SPANS), chord)
        return (span, lax.rem(chord + CHORDS + 2 * side - 1, CHORDS))

    def when_there(axis, side, act):
        place, count = ((span, SPANS), (chord, CHORDS))[axis]
        there = place + 2 * side
        pl.when(jnp.logical_and(there > 0, there <= count))(act)

    me_in = (chord * 2 + core, chip)

    def partner(phase, off):
        there = lax.rem(me_in[phase] + off, GROUP)
        if phase == 0:
            return (chip * 2 + lax.rem(there, 2), there // 2)
        return (there * 2 + core, chord)

    barrier = pltpu.get_barrier_semaphore()
    for side in (0, 1):
        pl.semaphore_signal(barrier, inc=1, device_id=neighbour(0, side), device_id_type=MESH)
    for phase in range(2):
        for off in range(1, GROUP):
            pl.semaphore_signal(
                barrier, inc=1, device_id=partner(phase, off), device_id_type=MESH
            )

    basis[...] = jnp.zeros_like(basis)
    adj[...] = jnp.zeros_like(adj)
    gacc[...] = jnp.zeros_like(gacc)
    for copy in small_copies[:2]:
        copy.wait()
    alive = lax.broadcasted_iota(jnp.int32, (8, ELEMS), 1) < live[0]
    alive6 = alive[:NVAR]
    lane6 = lax.broadcasted_iota(jnp.int32, (NVAR, ELEMS), 1)
    eye = lax.broadcasted_iota(jnp.int32, (GROUP, ELEMS), 0) == lax.broadcasted_iota(
        jnp.int32, (GROUP, ELEMS), 1
    )
    masks[0] = jnp.where(alive, 1.0, 0.0)
    vars6 = pl.ds(0, NVAR)
    for node in range(NODES):
        rows = pl.ds(node, NVAR, stride=NODES)
        basis[0, node, vars6, :] = jnp.where(alive6, rhs[rows, :], 0.0)
    for copy in small_copies[2:]:
        copy.wait()
    thetas = [shifts[order[k]] for k in range(STEPS)]

    def remote(step, axis, side):
        g, there = 2 * axis + side, 2 * axis + 1 - side
        return pltpu.make_async_remote_copy(
            src_ref=sbuf.at[step, g],
            dst_ref=rbuf.at[step, there],
            send_sem=send_sem.at[step, g],
            recv_sem=recv_sem.at[step, there],
            device_id=neighbour(axis, side),
            device_id_type=MESH,
        )

    def face_products(k, faces, first, unroll):
        def some(v, sums):
            sums = list(sums)
            for j in range(9):
                for n, (axis, side) in enumerate(faces):
                    g = 2 * axis + side
                    if first:
                        block = fstage[g, v * 9 + j].astype(F32)
                        face[g, v * 9 + j] = block
                    else:
                        block = face[g, v * 9 + j]
                    sums[n] = sums[n] + block * basis[k, node_of(axis, side, j), pl.ds(v, 1), :]
            return tuple(sums)

        def body(i, sums):
            for u in range(unroll):
                sums = some(i * unroll + u, sums)
            return sums

        zero = tuple(jnp.zeros((FACE, ELEMS), F32) for _ in faces)
        if unroll == NVAR:
            return body(0, zero)
        return lax.fori_loop(0, NVAR // unroll, body, zero)

    def oriented(g, product):
        prod[g, pl.ds(0, FACE), :] = product
        y = [[prod[g, pl.ds(3 * s + t, NVAR, stride=9), :] for t in range(3)] for s in range(3)]
        code = jnp.broadcast_to(codes[pl.ds(g, 1), :], (NVAR, ELEMS))
        swap, flip_s, flip_t = [(code & bit) != 0 for bit in (4, 1, 2)]
        y = [[y[s][t] if s == t else jnp.where(swap, y[t][s], y[s][t]) for t in range(3)] for s in range(3)]
        y = [[y[s][t] if s == 1 else jnp.where(flip_s, y[2 - s][t], y[s][t]) for t in range(3)] for s in range(3)]
        y = [[y[s][t] if t == 1 else jnp.where(flip_t, y[s][2 - t], y[s][t]) for t in range(3)] for s in range(3)]
        return [y[j // 3][j % 3] for j in range(9)]

    def send_face(step, k, axis, side, first):
        g = 2 * axis + side
        (product,) = face_products(k, ((axis, side),), first, 1 if first else NVAR)
        for j, value in enumerate(oriented(g, product)):
            sbuf[step, g, j] = value
        when_there(axis, side, lambda: remote(step, axis, side).start())

    def local_faces(k, first):
        products = face_products(k, ((2, 0), (2, 1)), first, 1 if first else 3)
        for j, value in enumerate(oriented(5, products[1])):
            local[0, j] = jnp.where(lane6 == 0, 0.0, pltpu.roll(value, 1, 1))
        for j, value in enumerate(oriented(4, products[0])):
            local[1, j] = jnp.where(lane6 == ELEMS - 1, 0.0, pltpu.roll(value, ELEMS - 1, 1))

    def diag_product(k, first):
        def body(v, total):
            if first:
                diag_copy(v).wait()
            for node in range(NODES):
                p = v * NODES + node
                if first:
                    block = dstage[p].astype(F32)
                    diag[p] = block
                else:
                    block = diag[p]
                total = total + block * basis[k, node, pl.ds(v, 1), :]
            return total

        result[...] = lax.fori_loop(0, NVAR, body, jnp.zeros((BLOCK, ELEMS), F32))

    def own_part(k, theta):
        for node in range(NODES):
            c = node % 3
            value = result[pl.ds(node, NVAR, stride=NODES), :]
            if c != 1:
                value = value + local[c // 2, node // 3]
            value = jnp.where(alive6, value, 0.0)
            basis[k + 1, node, vars6, :] = value - theta * basis[k, node, vars6, :]

    def arrive(step, to, axis, side):
        def act():
            remote(step, axis, 1 - side).wait_recv()
            mask = masks[1, vars6, :]
            for j in range(9):
                at = node_of(axis, side, j)
                got = rbuf[step, 2 * axis + side, j]
                basis[to, at, vars6, :] = basis[to, at, vars6, :] + mask * got

        when_there(axis, side, act)

    def sent(step):
        for one in (far, middle, outer, near):
            when_there(*one, remote(step, *one).wait_send)

    def phase_copy(cycle, phase, off, count=None):
        place = pl.ds(0, count) if count else me_in[phase]
        ref = slots.at[cycle, phase, place]
        return pltpu.make_async_remote_copy(
            src_ref=ref,
            dst_ref=ref,
            send_sem=gsend_sem.at[cycle, phase],
            recv_sem=grecv_sem.at[cycle, phase],
            device_id=partner(phase, off),
            device_id_type=MESH,
        )

    def send_phase(cycle, phase, row):
        slots[cycle, phase, me_in[phase]] = row
        for off in range(1, GROUP):
            phase_copy(cycle, phase, off).start()

    def take_phase(cycle, phase):
        copy = phase_copy(cycle, phase, 1, GROUP - 1)
        copy.wait_recv()
        copy.wait_send()
        return jnp.sum(slots[cycle, phase], axis=0)

    def start_gram(cycle):
        def body(i, sums):
            sums = list(sums)
            for u in range(3):
                v = [basis[k, i * 3 + u] for k in range(5)]
                for a in range(5):
                    for b in range(a, 5):
                        e = pair_index(a, b)
                        sums[e] = sums[e] + v[a] * v[b]
            return tuple(sums)

        sums = lax.fori_loop(
            0, NODES // 3, body, tuple(jnp.zeros((8, ELEMS), F32) for _ in range(ENTRIES))
        )
        for e in range(ENTRIES):
            gacc[pl.ds(8 * e, 8), :] = sums[e]
        part = gacc[pl.ds(0, GROUP, stride=8), :]
        for r in range(1, 8):
            part = part + gacc[pl.ds(r, GROUP, stride=8), :]
        column = jnp.sum(part, axis=1, keepdims=True)
        row = jnp.sum(jnp.where(eye, column, 0.0), axis=0, keepdims=True)
        send_phase(cycle, 0, row)

    def middle_gram(cycle):
        send_phase(cycle, 1, take_phase(cycle, 0))

    def end_gram(cycle):
        row = take_phase(cycle, 1)
        spread = jnp.sum(jnp.where(eye, row, 0.0), axis=1, keepdims=True)
        spread = jnp.broadcast_to(spread, (GROUP, ELEMS))
        gram = [
            [spread[pair_index(i, j):pair_index(i, j) + 1] for j in range(5)] for i in range(5)
        ]
        half = [[gram[i][k] * thetas[k] + gram[i][k + 1] for k in range(4)] for i in range(5)]
        normal = [[half[j][k] * thetas[j] + half[j + 1][k] for k in range(4)] for j in range(4)]
        target = [gram[j][0] * thetas[j] + gram[j + 1][0] for j in range(4)]
        low = [[None] * 4 for _ in range(4)]
        scaled = [[None] * 4 for _ in range(4)]
        inverse = [None] * 4
        for j in range(4):
            for i in range(j, 4):
                value = normal[i][j]
                for m in range(j):
                    value = value - low[j][m] * scaled[i][m]
                scaled[i][j] = value
            inverse[j] = 1.0 / scaled[j][j]
            for i in range(j + 1, 4):
                low[i][j] = scaled[i][j] * inverse[j]
        fore = []
        for i in range(4):
            value = target[i]
            for m in range(i):
                value = value - low[i][m] * fore[m]
            fore.append(value)
        weights = [None] * 4
        for i in reversed(range(4)):
            value = fore[i] * inverse[i]
            for m in range(i + 1, 4):
                value = value - low[m][i] * weights[m]
            weights[i] = value
        combined = [weights[0] * thetas[0]]
        for i in range(1, 4):
            combined.append(weights[i] * thetas[i] + weights[i - 1])
        combined.append(weights[3])
        lanes = lax.broadcasted_iota(jnp.int32, (1, ELEMS), 1)
        line = jnp.zeros((1, ELEMS), F32)
        for i in range(4):
            line = jnp.where(lanes == i, weights[i], line)
        coef_out[pl.ds(cycle, 1), :] = line[:, :STEPS]
        return weights, combined

    def next_cycle(cycle):
        weights, combined = end_gram(cycle)
        sets = [[1.0 - combined[0]] + [-value for value in combined[1:]]]
        for m in range(AHEAD):
            old = sets[-1]
            new = [None] * (len(old) + 1)
            for i, value in enumerate(old):
                here = value * (thetas[i % STEPS] - thetas[m])
                new[i] = here if new[i] is None else new[i] + here
                new[i + 1] = value
            sets.append(new)
        factor = jnp.broadcast_to(sets[AHEAD][-1], (8, ELEMS))
        masks[1] = masks[0] * factor
        weights8, combined8 = wide(weights), wide(combined)
        sets8 = [wide(one) for one in sets[1:]]

        def body(i, carry):
            for u in range(3):
                at = i * 3 + u
                v = [basis[k, at] for k in range(STEPS + AHEAD + 1)]
                total = adj[at]
                for k in range(STEPS):
                    total = total + weights8[k] * v[k]
                adj[at] = total
                fresh = v[0]
                for k in range(STEPS + 1):
                    fresh = fresh - combined8[k] * v[k]
                basis[0, at] = fresh
                for m in range(AHEAD):
                    total = sets8[m][0] * v[0]
                    for k in range(1, len(sets8[m])):
                        total = total + sets8[m][k] * v[k]
                    basis[m + 1, at] = total
            return carry

        lax.fori_loop(0, NODES // 3, body, 0)

    def last_cycle(cycle):
        weights, combined = end_gram(cycle)
        weights6, combined6 = wide(weights, NVAR), wide(combined, NVAR)
        for node in range(NODES):
            rows = pl.ds(node, NVAR, stride=NODES)
            v = [basis[k, node, vars6, :] for k in range(STEPS + 1)]
            total = adj[node, vars6, :]
            for k in range(STEPS):
                total = total + weights6[k] * v[k]
            adj_out[rows, :] = total
            fresh = v[0]
            for k in range(STEPS + 1):
                fresh = fresh - combined6[k] * v[k]
            res_out[rows, :] = fresh

    def product(step, k, theta, first):
        for one in (far, middle, outer, near):
            if first:
                face_copy(*one).wait()
            if first and one is far:
                pl.semaphore_wait(barrier, 2 * GROUP)
            send_face(step, k, *one, first)
        to = k + 1
        if not first:
            sent(step - 1)
            place = lax.rem(step, 4)
            cycle = step // 4 - 1

            @pl.when(jnp.logical_and(place == 0, step >= STEPS))
            def _():
                start_gram(cycle)

        else:
            face_copy(2, 0).wait()
            face_copy(2, 1).wait()
        local_faces(k, first)
        diag_product(k, first)
        own_part(k, theta)
        masks[1] = masks[0]
        if not first:

            @pl.when(jnp.logical_and(place == 1, step >= STEPS))
            def _():
                middle_gram(cycle)

            @pl.when(jnp.logical_and(place == 3, step >= STEPS))
            def _():
                next_cycle(cycle)

            to = jnp.where(k == STEPS + AHEAD - 1, AHEAD, to)
        for one in (near, outer, middle, far):
            arrive(step, to, *one)

    product(0, 0, thetas[0], True)

    def step_body(step, carry):
        k = jnp.where(step < STEPS, step, lax.rem(step, STEPS) + STEPS)
        product(step, k, shifts[order[lax.rem(k, STEPS)]], False)
        return carry

    lax.fori_loop(1, TOTAL, step_body, 0)
    start_gram(CYCLES - 1)
    sent(TOTAL - 1)
    middle_gram(CYCLES - 1)
    last_cycle(CYCLES - 1)


def wide(values, rows=8):
    return [jnp.broadcast_to(value, (rows, ELEMS)) for value in values]


def copy_kernel(a, b, c, x, y, z):
    x[...] = a[...]
    y[...] = b[...]
    z[...] = c[...]


def hand_out(arrays):
    vmem = pl.BlockSpec(memory_space=pltpu.VMEM)
    return pl.pallas_call(
        copy_kernel,
        out_shape=tuple(jax.ShapeDtypeStruct(one.shape, one.dtype) for one in arrays),
        in_specs=[vmem] * 3,
        out_specs=(vmem,) * 3,
    )(*arrays)


def on_device(right_side, diag_blocks, face_blocks, orient_codes, live_counts, shifts, shift_order):
    vmem = pl.BlockSpec(memory_space=pltpu.VMEM)
    anywhere = pl.BlockSpec(memory_space=pl.ANY)
    arrays = pl.pallas_call(
        kernel,
        out_shape=(
            jax.ShapeDtypeStruct((BLOCK, ELEMS), F32),
            jax.ShapeDtypeStruct((BLOCK, ELEMS), F32),
            jax.ShapeDtypeStruct((CYCLES, STEPS), F32),
        ),
        in_specs=[anywhere] * 7,
        out_specs=(vmem, vmem, vmem),
        scratch_shapes=[
            pltpu.VMEM((BLOCK, BLOCK, ELEMS), jnp.bfloat16),
            pltpu.VMEM((6, FACE, FACE, ELEMS), jnp.bfloat16),
            pltpu.VMEM((BLOCK, BLOCK, ELEMS), F32),
            pltpu.VMEM((6, FACE, FACE, ELEMS), F32),
            pltpu.VMEM((BLOCK, ELEMS), F32),
            pltpu.VMEM((6, ELEMS), jnp.int32),
            pltpu.SMEM((1,), jnp.int32),
            pltpu.SMEM((STEPS,), F32),
            pltpu.SMEM((STEPS,), jnp.int32),
            pltpu.VMEM((STEPS + AHEAD + 1, NODES, 8, ELEMS), F32),
            pltpu.VMEM((NODES, 8, ELEMS), F32),
            pltpu.VMEM((6, 56, ELEMS), F32),
            pltpu.VMEM((BLOCK, ELEMS), F32),
            pltpu.VMEM((2, 9, NVAR, ELEMS), F32),
            pltpu.VMEM((2, 8, ELEMS), F32),
            pltpu.VMEM((TOTAL, 4, 9, NVAR, ELEMS), F32),
            pltpu.VMEM((TOTAL, 4, 9, NVAR, ELEMS), F32),
            pltpu.VMEM((GROUP * 8, ELEMS), F32),
            pltpu.VMEM((CYCLES, 2, GROUP, 1, ELEMS), F32),
            pltpu.SemaphoreType.DMA((5,)),
            pltpu.SemaphoreType.DMA((BLOCK // CHUNK,)),
            pltpu.SemaphoreType.DMA((6,)),
            pltpu.SemaphoreType.DMA((TOTAL, 4)),
            pltpu.SemaphoreType.DMA((TOTAL, 4)),
            pltpu.SemaphoreType.DMA((CYCLES, 2)),
            pltpu.SemaphoreType.DMA((CYCLES, 2)),
        ],
        compiler_params=pltpu.CompilerParams(
            collective_id=0, has_side_effects=True, vmem_limit_bytes=56 * 2**20
        ),
    )(right_side, diag_blocks, face_blocks, orient_codes, live_counts, shifts, shift_order)
    return hand_out(arrays)


def solution(mesh):
    placed = (
        P(None, ("span", "chord")),
        P(None, None, ("span", "chord")),
        P(None, None, None, ("span", "chord")),
        P(None, ("span", "chord")),
        P(("span", "chord")),
        P(),
        P(),
    )
    return jax.shard_map(
        on_device,
        mesh=mesh,
        in_specs=placed,
        out_specs=(P(None, ("span", "chord")), P(None, ("span", "chord")), P()),
        check_vma=False,
    )
```

```python
import functools

import jax
import jax.numpy as jnp
from jax import lax
from jax.experimental import pallas as pl
from jax.experimental.pallas import tpu as pltpu
from jax.sharding import PartitionSpec as P

MESH = pl.DeviceIdType.MESH
F32 = jnp.float32

CYCLES = 3
STEPS = 4
AHEAD = 4
TOTAL = 12
BLOCK = 162
FACE = 54
NVAR = 6
NODES = 27
WIDE = 8 * NODES
ELEMS = 128
SPANS = 32
CHORDS = 8
GROUP = 16
ENTRIES = 15
CHUNK = 27

def node_of(axis, side, j):
    if axis == 0:
        return side * 18 + j
    if axis == 1:
        return (j // 3) * 9 + side * 6 + j % 3
    return j * 3 + side * 2


def pair_index(i, j):
    i, j = min(i, j), max(i, j)
    return i * 5 - i * (i - 1) // 2 + (j - i)


def kernel(
    rhs_hbm, diag_hbm, face_hbm, codes_hbm, live_hbm, shifts_hbm, order_hbm,
    adj_out, res_out, coef_out,
    dstage, fstage, face, rhs, codes, live, shifts, order, basis, adj, prod, result, local, masks, sbuf, rbuf,
    gacc, slots, lines, done,
    small_sem, dsem, fsem, send_sem, recv_sem, gsend_sem, grecv_sem,
):
    span, chord = lax.axis_index("span"), lax.axis_index("chord")
    core, chip = lax.rem(span, 2), span // 2
    inner = (chord < CHORDS // 2).astype(jnp.int32)
    far, middle, outer, near = (0, core), (1, inner), (1, 1 - inner), (0, 1 - core)

    small_copies = [
        pltpu.make_async_copy(source, target, small_sem.at[i])
        for i, (source, target) in enumerate(
            (
                (rhs_hbm, rhs.at[pl.ds(0, BLOCK)]),
                (live_hbm, live),
                (codes_hbm, codes.at[pl.ds(0, 6)]),
                (shifts_hbm, shifts),
                (order_hbm, order),
            )
        )
    ]
    for copy in small_copies[:2]:
        copy.start()

    def face_copy(axis, side):
        g = 2 * axis + side
        return pltpu.make_async_copy(face_hbm.at[g], fstage.at[g], fsem.at[g])

    face_copy(*middle).start()

    def neighbour(axis, side):
        if axis == 0:
            return (lax.rem(span + SPANS + 2 * side - 1, SPANS), chord)
        return (span, lax.rem(chord + CHORDS + 2 * side - 1, CHORDS))

    def when_there(axis, side, act):
        place, count = ((span, SPANS), (chord, CHORDS))[axis]
        there = place + 2 * side
        pl.when(jnp.logical_and(there > 0, there <= count))(act)

    me_in = (chord * 2 + core, chip)

    def partner(phase, off):
        there = lax.rem(me_in[phase] + off, GROUP)
        if phase == 0:
            return (chip * 2 + lax.rem(there, 2), there // 2)
        return (there * 2 + core, chord)

    barrier = pltpu.get_barrier_semaphore()
    for side in (0, 1):
        pl.semaphore_signal(barrier, inc=1, device_id=neighbour(0, side), device_id_type=MESH)
    for phase in range(2):
        for off in range(1, GROUP):
            pl.semaphore_signal(
                barrier, inc=1, device_id=partner(phase, off), device_id_type=MESH
            )

    for copy in small_copies[2:]:
        copy.start()
    for one in (far, outer, near, (2, 0), (2, 1)):
        face_copy(*one).start()

    def diag_copy(i):
        rows = pl.ds(i * CHUNK, CHUNK)
        return pltpu.make_async_copy(diag_hbm.at[rows], dstage.at[rows], dsem.at[i])

    for i in range(BLOCK // CHUNK):
        diag_copy(i).start()

    basis[...] = jnp.zeros_like(basis)
    adj[...] = jnp.zeros_like(adj)
    gacc[...] = jnp.zeros_like(gacc)
    for copy in small_copies[:2]:
        copy.wait()
    alive = lax.broadcasted_iota(jnp.int32, (8, ELEMS), 1) < live[0]
    alive6 = alive[:NVAR]
    lane6 = lax.broadcasted_iota(jnp.int32, (NVAR, ELEMS), 1)
    eye = lax.broadcasted_iota(jnp.int32, (GROUP, ELEMS), 0) == lax.broadcasted_iota(
        jnp.int32, (GROUP, ELEMS), 1
    )
    masks[0] = jnp.where(alive, 1.0, 0.0)
    vars6 = pl.ds(0, NVAR)
    for node in range(NODES):
        rows = pl.ds(node, NVAR, stride=NODES)
        basis[0, node, vars6, :] = jnp.where(alive6, rhs[rows, :], 0.0)
    for copy in small_copies[2:]:
        copy.wait()
    thetas = [shifts[order[k]] for k in range(STEPS)]

    def remote(step, axis, side):
        g, there = 2 * axis + side, 2 * axis + 1 - side
        return pltpu.make_async_remote_copy(
            src_ref=sbuf.at[step, g],
            dst_ref=rbuf.at[step, there],
            send_sem=send_sem.at[step, g],
            recv_sem=recv_sem.at[step, there],
            device_id=neighbour(axis, side),
            device_id_type=MESH,
        )

    def face_products(k, faces, first, unroll, slot=None):
        def some(v, sums):
            sums = list(sums)
            for j in range(9):
                for n, (axis, side) in enumerate(faces):
                    g = 2 * axis + side
                    if slot is not None and not first:
                        block = face[slot, v * 9 + j]
                    else:
                        block = fstage[g, v * 9 + j].astype(F32)
                        if slot is not None:
                            face[slot, v * 9 + j] = block
                    sums[n] = sums[n] + block * basis[k, node_of(axis, side, j), pl.ds(v, 1), :]
            return tuple(sums)

        def body(i, sums):
            for u in range(unroll):
                sums = some(i * unroll + u, sums)
            return sums

        zero = tuple(jnp.zeros((FACE, ELEMS), F32) for _ in faces)
        if unroll == NVAR:
            return body(0, zero)
        return lax.fori_loop(0, NVAR // unroll, body, zero)

    def oriented(g, product):
        prod[g, pl.ds(0, FACE), :] = product
        y = [[prod[g, pl.ds(3 * s + t, NVAR, stride=9), :] for t in range(3)] for s in range(3)]
        code = jnp.broadcast_to(codes[pl.ds(g, 1), :], (NVAR, ELEMS))
        swap, flip_s, flip_t = [(code & bit) != 0 for bit in (4, 1, 2)]
        y = [[y[s][t] if s == t else jnp.where(swap, y[t][s], y[s][t]) for t in range(3)] for s in range(3)]
        y = [[y[s][t] if s == 1 else jnp.where(flip_s, y[2 - s][t], y[s][t]) for t in range(3)] for s in range(3)]
        y = [[y[s][t] if t == 1 else jnp.where(flip_t, y[s][2 - t], y[s][t]) for t in range(3)] for s in range(3)]
        return [y[j // 3][j % 3] for j in range(9)]

    def send_face(step, k, axis, side, first, slot):
        g = 2 * axis + side
        (product,) = face_products(k, ((axis, side),), first, NVAR, slot)
        for j, value in enumerate(oriented(g, product)):
            sbuf[step, g, j] = value
        if first and slot == 0:
            pl.semaphore_wait(barrier, 2 * GROUP)
        when_there(axis, side, lambda: remote(step, axis, side).start())

    def local_faces(k, first):
        products = face_products(k, ((2, 0), (2, 1)), first, 3)
        for j, value in enumerate(oriented(5, products[1])):
            local[0, j] = jnp.where(lane6 == 0, 0.0, pltpu.roll(value, 1, 1))
        for j, value in enumerate(oriented(4, products[0])):
            local[1, j] = jnp.where(lane6 == ELEMS - 1, 0.0, pltpu.roll(value, ELEMS - 1, 1))

    def diag_product(k, first):
        def body(v, total):
            if first:
                diag_copy(v).wait()
            for node in range(NODES):
                p = v * NODES + node
                block = dstage[p].astype(F32)
                total = total + block * basis[k, node, pl.ds(v, 1), :]
            return total

        result[pl.ds(0, BLOCK), :] = lax.fori_loop(0, NVAR, body, jnp.zeros((BLOCK, ELEMS), F32))

    def own_part(k, theta):
        for node in range(NODES):
            c = node % 3
            value = result[pl.ds(node, NVAR, stride=NODES), :]
            if c != 1:
                value = value + local[c // 2, node // 3]
            value = jnp.where(alive6, value, 0.0)
            basis[k + 1, node, vars6, :] = value - theta * basis[k, node, vars6, :]

    def arrive(step, to, axis, side):
        def act():
            remote(step, axis, 1 - side).wait_recv()
            mask = masks[1, vars6, :]
            for j in range(9):
                at = node_of(axis, side, j)
                got = rbuf[step, 2 * axis + side, j]
                basis[to, at, vars6, :] = basis[to, at, vars6, :] + mask * got

        when_there(axis, side, act)

    def sent(step):
        for one in (far, middle, outer, near):
            when_there(*one, remote(step, *one).wait_send)

    def phase_copy(cycle, phase, off, count=None):
        place = pl.ds(0, count) if count else me_in[phase]
        ref = slots.at[cycle, phase, place]
        return pltpu.make_async_remote_copy(
            src_ref=ref,
            dst_ref=ref,
            send_sem=gsend_sem.at[cycle, phase],
            recv_sem=grecv_sem.at[cycle, phase],
            device_id=partner(phase, off),
            device_id_type=MESH,
        )

    def send_phase(cycle, phase, row):
        slots[cycle, phase, me_in[phase]] = row
        for off in range(1, GROUP):
            phase_copy(cycle, phase, off).start()

    def take_phase(cycle, phase):
        copy = phase_copy(cycle, phase, 1, GROUP - 1)
        copy.wait_recv()
        copy.wait_send()
        return jnp.sum(slots[cycle, phase], axis=0)

    def start_gram(cycle):
        def body(i, sums):
            sums = list(sums)
            for u in range(3):
                v = [basis[k, i * 3 + u] for k in range(5)]
                for a in range(5):
                    for b in range(a, 5):
                        e = pair_index(a, b)
                        sums[e] = sums[e] + v[a] * v[b]
            return tuple(sums)

        sums = lax.fori_loop(
            0, NODES // 3, body, tuple(jnp.zeros((8, ELEMS), F32) for _ in range(ENTRIES))
        )
        for e in range(ENTRIES):
            gacc[pl.ds(8 * e, 8), :] = sums[e]
        part = gacc[pl.ds(0, GROUP, stride=8), :]
        for r in range(1, 8):
            part = part + gacc[pl.ds(r, GROUP, stride=8), :]
        column = jnp.sum(part, axis=1, keepdims=True)
        row = jnp.sum(jnp.where(eye, column, 0.0), axis=0, keepdims=True)
        send_phase(cycle, 0, row)

    def middle_gram(cycle):
        send_phase(cycle, 1, take_phase(cycle, 0))

    def end_gram(cycle):
        row = take_phase(cycle, 1)
        spread = jnp.sum(jnp.where(eye, row, 0.0), axis=1, keepdims=True)
        spread = jnp.broadcast_to(spread, (GROUP, ELEMS))
        gram = [
            [spread[pair_index(i, j):pair_index(i, j) + 1] for j in range(5)] for i in range(5)
        ]
        half = [[gram[i][k] * thetas[k] + gram[i][k + 1] for k in range(4)] for i in range(5)]
        normal = [[half[j][k] * thetas[j] + half[j + 1][k] for k in range(4)] for j in range(4)]
        target = [gram[j][0] * thetas[j] + gram[j + 1][0] for j in range(4)]
        low = [[None] * 4 for _ in range(4)]
        scaled = [[None] * 4 for _ in range(4)]
        inverse = [None] * 4
        for j in range(4):
            for i in range(j, 4):
                value = normal[i][j]
                for m in range(j):
                    value = value - low[j][m] * scaled[i][m]
                scaled[i][j] = value
            inverse[j] = 1.0 / scaled[j][j]
            for i in range(j + 1, 4):
                low[i][j] = scaled[i][j] * inverse[j]
        fore = []
        for i in range(4):
            value = target[i]
            for m in range(i):
                value = value - low[i][m] * fore[m]
            fore.append(value)
        weights = [None] * 4
        for i in reversed(range(4)):
            value = fore[i] * inverse[i]
            for m in range(i + 1, 4):
                value = value - low[m][i] * weights[m]
            weights[i] = value
        combined = [weights[0] * thetas[0]]
        for i in range(1, 4):
            combined.append(weights[i] * thetas[i] + weights[i - 1])
        combined.append(weights[3])
        lanes = lax.broadcasted_iota(jnp.int32, (1, ELEMS), 1)
        line = jnp.zeros((1, ELEMS), F32)
        for i in range(4):
            line = jnp.where(lanes == i, weights[i], line)
        lines[pl.ds(cycle, 1), :] = line
        return weights, combined

    def next_cycle(cycle):
        weights, combined = end_gram(cycle)
        sets = [[1.0 - combined[0]] + [-value for value in combined[1:]]]
        for m in range(AHEAD):
            old = sets[-1]
            new = [None] * (len(old) + 1)
            for i, value in enumerate(old):
                here = value * (thetas[i % STEPS] - thetas[m])
                new[i] = here if new[i] is None else new[i] + here
                new[i + 1] = value
            sets.append(new)
        factor = jnp.broadcast_to(sets[AHEAD][-1], (8, ELEMS))
        masks[1] = masks[0] * factor
        weights8, combined8 = wide(weights), wide(combined)
        sets8 = [wide(one) for one in sets[1:]]

        def body(i, carry):
            for u in range(3):
                at = i * 3 + u
                v = [basis[k, at] for k in range(STEPS + AHEAD + 1)]
                total = adj[at]
                for k in range(STEPS):
                    total = total + weights8[k] * v[k]
                adj[at] = total
                fresh = v[0]
                for k in range(STEPS + 1):
                    fresh = fresh - combined8[k] * v[k]
                basis[0, at] = fresh
                for m in range(AHEAD):
                    total = sets8[m][0] * v[0]
                    for k in range(1, len(sets8[m])):
                        total = total + sets8[m][k] * v[k]
                    basis[m + 1, at] = total
            return carry

        lax.fori_loop(0, NODES // 3, body, 0)

    def last_cycle(cycle):
        weights, combined = end_gram(cycle)
        weights6, combined6 = wide(weights, NVAR), wide(combined, NVAR)
        for node in range(NODES):
            rows = pl.ds(node, NVAR, stride=NODES)
            v = [basis[k, node, vars6, :] for k in range(STEPS + 1)]
            total = adj[node, vars6, :]
            for k in range(STEPS):
                total = total + weights6[k] * v[k]
            done[0, rows, :] = total
            fresh = v[0]
            for k in range(STEPS + 1):
                fresh = fresh - combined6[k] * v[k]
            done[1, rows, :] = fresh

        adj_out[...] = done[0, pl.ds(0, BLOCK), :]
        res_out[...] = done[1, pl.ds(0, BLOCK), :]
        coef_out[...] = lines[pl.ds(0, CYCLES), :][:, :STEPS]

    def product(step, k, theta, first):
        for slot, one in ((0, middle), (1, far), (None, outer), (None, near)):
            if first:
                face_copy(*one).wait()
            send_face(step, k, *one, first, slot)
        to = k + 1
        if not first:
            sent(step - 1)
            place = lax.rem(step, 4)
            cycle = step // 4 - 1

            @pl.when(jnp.logical_and(place == 0, step >= STEPS))
            def _():
                start_gram(cycle)

        else:
            face_copy(2, 0).wait()
            face_copy(2, 1).wait()
        local_faces(k, first)
        diag_product(k, first)
        own_part(k, theta)
        masks[1] = masks[0]
        if not first:

            @pl.when(jnp.logical_and(place == 1, step >= STEPS))
            def _():
                middle_gram(cycle)

            @pl.when(jnp.logical_and(place == 3, step >= STEPS))
            def _():
                next_cycle(cycle)

            to = jnp.where(k == STEPS + AHEAD - 1, AHEAD, to)
        for one in (near, outer, far, middle):
            arrive(step, to, *one)

    product(0, 0, thetas[0], True)

    def step_body(step, carry):
        k = jnp.where(step < STEPS, step, lax.rem(step, STEPS) + STEPS)
        product(step, k, shifts[order[lax.rem(k, STEPS)]], False)
        return carry

    lax.fori_loop(1, TOTAL, step_body, 0)
    start_gram(CYCLES - 1)
    sent(TOTAL - 1)
    middle_gram(CYCLES - 1)
    last_cycle(CYCLES - 1)


def wide(values, rows=8):
    return [jnp.broadcast_to(value, (rows, ELEMS)) for value in values]


def copy_kernel(a, b, c, x, y, z):
    x[...] = a[...]
    y[...] = b[...]
    z[...] = c[...]


def hand_out(arrays):
    vmem = pl.BlockSpec(memory_space=pltpu.VMEM)
    return pl.pallas_call(
        copy_kernel,
        out_shape=tuple(jax.ShapeDtypeStruct(one.shape, one.dtype) for one in arrays),
        in_specs=[vmem] * 3,
        out_specs=(vmem,) * 3,
    )(*arrays)


def on_device(right_side, diag_blocks, face_blocks, orient_codes, live_counts, shifts, shift_order):
    vmem = pl.BlockSpec(memory_space=pltpu.VMEM)
    hbm = pl.BlockSpec(memory_space=pltpu.HBM)
    arrays = pl.pallas_call(
        kernel,
        out_shape=(
            jax.ShapeDtypeStruct((BLOCK, ELEMS), F32),
            jax.ShapeDtypeStruct((BLOCK, ELEMS), F32),
            jax.ShapeDtypeStruct((CYCLES, STEPS), F32),
        ),
        in_specs=[hbm] * 7,
        out_specs=(vmem, vmem, vmem),
        scratch_shapes=[
            pltpu.VMEM((BLOCK, BLOCK, ELEMS), jnp.bfloat16),
            pltpu.VMEM((6, FACE, FACE, ELEMS), jnp.bfloat16),
            pltpu.VMEM((2, FACE, FACE, ELEMS), F32),
            pltpu.VMEM((WIDE, ELEMS), F32),
            pltpu.VMEM((16, ELEMS), jnp.int32),
            pltpu.SMEM((1,), jnp.int32),
            pltpu.SMEM((STEPS,), F32),
            pltpu.SMEM((STEPS,), jnp.int32),
            pltpu.VMEM((STEPS + AHEAD + 1, NODES, 8, ELEMS), F32),
            pltpu.VMEM((NODES, 8, ELEMS), F32),
            pltpu.VMEM((6, 72, ELEMS), F32),
            pltpu.VMEM((WIDE, ELEMS), F32),
            pltpu.VMEM((2, 9, NVAR, ELEMS), F32),
            pltpu.VMEM((2, 8, ELEMS), F32),
            pltpu.VMEM((TOTAL, 4, 9, NVAR, ELEMS), F32),
            pltpu.VMEM((TOTAL, 4, 9, NVAR, ELEMS), F32),
            pltpu.VMEM((GROUP * 8, ELEMS), F32),
            pltpu.VMEM((CYCLES + 1, 2, GROUP, 1, ELEMS), F32),
            pltpu.VMEM((16, ELEMS), F32),
            pltpu.VMEM((2, WIDE, ELEMS), F32),
            pltpu.SemaphoreType.DMA((5,)),
            pltpu.SemaphoreType.DMA((BLOCK // CHUNK,)),
            pltpu.SemaphoreType.DMA((6,)),
            pltpu.SemaphoreType.DMA((TOTAL, 4)),
            pltpu.SemaphoreType.DMA((TOTAL, 4)),
            pltpu.SemaphoreType.DMA((CYCLES, 2)),
            pltpu.SemaphoreType.DMA((CYCLES, 2)),
        ],
        compiler_params=pltpu.CompilerParams(
            collective_id=0, has_side_effects=True, vmem_limit_bytes=56 * 2**20
        ),
    )(right_side, diag_blocks, face_blocks, orient_codes, live_counts, shifts, shift_order)
    return hand_out(arrays)


def solution(mesh):
    placed = (
        P(None, ("span", "chord")),
        P(None, None, ("span", "chord")),
        P(None, None, None, ("span", "chord")),
        P(None, ("span", "chord")),
        P(("span", "chord")),
        P(),
        P(),
    )
    return jax.shard_map(
        on_device,
        mesh=mesh,
        in_specs=placed,
        out_specs=(P(None, ("span", "chord")), P(None, ("span", "chord")), P()),
        check_vma=False,
    )
```

```python
import functools

import jax
import jax.numpy as jnp
from jax import lax
from jax.experimental import pallas as pl
from jax.experimental.pallas import tpu as pltpu
from jax.sharding import PartitionSpec as P

MESH = pl.DeviceIdType.MESH
F32 = jnp.float32

CYCLES = 3
STEPS = 4
AHEAD = 4
TOTAL = 12
BLOCK = 162
FACE = 54
NVAR = 6
NODES = 27
WIDE = 8 * NODES
ELEMS = 128
SPANS = 32
CHORDS = 8
GROUP = 16
ENTRIES = 15
CHUNK = 27

def node_of(axis, side, j):
    if axis == 0:
        return side * 18 + j
    if axis == 1:
        return (j // 3) * 9 + side * 6 + j % 3
    return j * 3 + side * 2


def pair_index(i, j):
    i, j = min(i, j), max(i, j)
    return i * 5 - i * (i - 1) // 2 + (j - i)


def kernel(
    rhs_hbm, diag_hbm, face_hbm, codes_hbm, live_hbm, shifts_hbm, order_hbm,
    adj_out, res_out, coef_out,
    dstage, fstage, face, rhs, codes, live, shifts, order, basis, adj, prod, result, local, masks, sbuf, rbuf,
    gacc, slots, lines, done,
    small_sem, dsem, fsem, send_sem, recv_sem, gsend_sem, grecv_sem,
):
    span, chord = lax.axis_index("span"), lax.axis_index("chord")
    core, chip = lax.rem(span, 2), span // 2
    inner = (chord < CHORDS // 2).astype(jnp.int32)
    far, middle, outer, near = (0, core), (1, inner), (1, 1 - inner), (0, 1 - core)

    small_copies = [
        pltpu.make_async_copy(source, target, small_sem.at[i])
        for i, (source, target) in enumerate(
            (
                (rhs_hbm, rhs.at[pl.ds(0, BLOCK)]),
                (live_hbm, live),
                (codes_hbm, codes.at[pl.ds(0, 6)]),
                (shifts_hbm, shifts),
                (order_hbm, order),
            )
        )
    ]
    for copy in small_copies[:2]:
        copy.start()

    def face_copy(axis, side):
        g = 2 * axis + side
        return pltpu.make_async_copy(face_hbm.at[g], fstage.at[g], fsem.at[g])

    face_copy(*middle).start()

    def neighbour(axis, side):
        if axis == 0:
            return (lax.rem(span + SPANS + 2 * side - 1, SPANS), chord)
        return (span, lax.rem(chord + CHORDS + 2 * side - 1, CHORDS))

    def when_there(axis, side, act):
        place, count = ((span, SPANS), (chord, CHORDS))[axis]
        there = place + 2 * side
        pl.when(jnp.logical_and(there > 0, there <= count))(act)

    me_in = (chord * 2 + core, chip)

    def partner(phase, off):
        there = lax.rem(me_in[phase] + off, GROUP)
        if phase == 0:
            return (chip * 2 + lax.rem(there, 2), there // 2)
        return (there * 2 + core, chord)

    barrier = pltpu.get_barrier_semaphore()
    for side in (0, 1):
        pl.semaphore_signal(barrier, inc=1, device_id=neighbour(0, side), device_id_type=MESH)
    for phase in range(2):
        for off in range(1, GROUP):
            pl.semaphore_signal(
                barrier, inc=1, device_id=partner(phase, off), device_id_type=MESH
            )

    for copy in small_copies[2:]:
        copy.start()
    for one in (far, outer, near, (2, 0), (2, 1)):
        face_copy(*one).start()

    def diag_copy(i):
        rows = pl.ds(i * CHUNK, CHUNK)
        return pltpu.make_async_copy(diag_hbm.at[rows], dstage.at[rows], dsem.at[i])

    for i in range(BLOCK // CHUNK):
        diag_copy(i).start()

    basis[...] = jnp.zeros_like(basis)
    adj[...] = jnp.zeros_like(adj)
    gacc[...] = jnp.zeros_like(gacc)
    for copy in small_copies[:2]:
        copy.wait()
    alive = lax.broadcasted_iota(jnp.int32, (8, ELEMS), 1) < live[0]
    alive6 = alive[:NVAR]
    lane6 = lax.broadcasted_iota(jnp.int32, (NVAR, ELEMS), 1)
    eye = lax.broadcasted_iota(jnp.int32, (GROUP, ELEMS), 0) == lax.broadcasted_iota(
        jnp.int32, (GROUP, ELEMS), 1
    )
    masks[0] = jnp.where(alive, 1.0, 0.0)
    vars6 = pl.ds(0, NVAR)
    for node in range(NODES):
        rows = pl.ds(node, NVAR, stride=NODES)
        basis[0, node, vars6, :] = jnp.where(alive6, rhs[rows, :], 0.0)
    for copy in small_copies[2:]:
        copy.wait()
    thetas = [shifts[order[k]] for k in range(STEPS)]

    def remote(step, axis, side):
        g, there = 2 * axis + side, 2 * axis + 1 - side
        return pltpu.make_async_remote_copy(
            src_ref=sbuf.at[step, g],
            dst_ref=rbuf.at[step, there],
            send_sem=send_sem.at[step, g],
            recv_sem=recv_sem.at[step, there],
            device_id=neighbour(axis, side),
            device_id_type=MESH,
        )

    def face_products(k, faces, first, unroll, slot=None):
        def some(v, sums):
            sums = list(sums)
            for j in range(9):
                for n, (axis, side) in enumerate(faces):
                    g = 2 * axis + side
                    if slot is not None and not first:
                        block = face[slot, v * 9 + j]
                    else:
                        block = fstage[g, v * 9 + j].astype(F32)
                        if slot is not None:
                            face[slot, v * 9 + j] = block
                    sums[n] = sums[n] + block * basis[k, node_of(axis, side, j), pl.ds(v, 1), :]
            return tuple(sums)

        def body(i, sums):
            for u in range(unroll):
                sums = some(i * unroll + u, sums)
            return sums

        zero = tuple(jnp.zeros((FACE, ELEMS), F32) for _ in faces)
        if unroll == NVAR:
            return body(0, zero)
        return lax.fori_loop(0, NVAR // unroll, body, zero)

    def oriented(g, product):
        prod[g, pl.ds(0, FACE), :] = product
        y = [[prod[g, pl.ds(3 * s + t, NVAR, stride=9), :] for t in range(3)] for s in range(3)]
        code = jnp.broadcast_to(codes[pl.ds(g, 1), :], (NVAR, ELEMS))
        swap, flip_s, flip_t = [(code & bit) != 0 for bit in (4, 1, 2)]
        y = [[y[s][t] if s == t else jnp.where(swap, y[t][s], y[s][t]) for t in range(3)] for s in range(3)]
        y = [[y[s][t] if s == 1 else jnp.where(flip_s, y[2 - s][t], y[s][t]) for t in range(3)] for s in range(3)]
        y = [[y[s][t] if t == 1 else jnp.where(flip_t, y[s][2 - t], y[s][t]) for t in range(3)] for s in range(3)]
        return [y[j // 3][j % 3] for j in range(9)]

    def send_face(step, k, axis, side, first, slot):
        g = 2 * axis + side
        (product,) = face_products(k, ((axis, side),), first, NVAR, slot)
        for j, value in enumerate(oriented(g, product)):
            sbuf[step, g, j] = value
        if first and slot == 0:
            pl.semaphore_wait(barrier, 2 * GROUP)
        when_there(axis, side, lambda: remote(step, axis, side).start())

    def local_faces(k, first):
        products = face_products(k, ((2, 0), (2, 1)), first, 3)
        for j, value in enumerate(oriented(5, products[1])):
            local[0, j] = jnp.where(lane6 == 0, 0.0, pltpu.roll(value, 1, 1))
        for j, value in enumerate(oriented(4, products[0])):
            local[1, j] = jnp.where(lane6 == ELEMS - 1, 0.0, pltpu.roll(value, ELEMS - 1, 1))

    def diag_product(k, first):
        def body(v, total):
            if first:
                diag_copy(v).wait()
            for node in range(NODES):
                p = v * NODES + node
                block = dstage[p].astype(F32)
                total = total + block * basis[k, node, pl.ds(v, 1), :]
            return total

        result[pl.ds(0, BLOCK), :] = lax.fori_loop(0, NVAR, body, jnp.zeros((BLOCK, ELEMS), F32))

    def own_part(k, theta):
        for node in range(NODES):
            c = node % 3
            value = result[pl.ds(node, NVAR, stride=NODES), :]
            if c != 1:
                value = value + local[c // 2, node // 3]
            value = jnp.where(alive6, value, 0.0)
            basis[k + 1, node, vars6, :] = value - theta * basis[k, node, vars6, :]

    def arrive(step, to, axis, side):
        def act():
            remote(step, axis, 1 - side).wait_recv()
            mask = masks[1, vars6, :]
            for j in range(9):
                at = node_of(axis, side, j)
                got = rbuf[step, 2 * axis + side, j]
                basis[to, at, vars6, :] = basis[to, at, vars6, :] + mask * got

        when_there(axis, side, act)

    def sent(step):
        for one in (far, middle, outer, near):
            when_there(*one, remote(step, *one).wait_send)

    def phase_copy(cycle, phase, off, count=None):
        place = pl.ds(0, count) if count else me_in[phase]
        ref = slots.at[cycle, phase, place]
        return pltpu.make_async_remote_copy(
            src_ref=ref,
            dst_ref=ref,
            send_sem=gsend_sem.at[cycle, phase],
            recv_sem=grecv_sem.at[cycle, phase],
            device_id=partner(phase, off),
            device_id_type=MESH,
        )

    def send_phase(cycle, phase, row):
        slots[cycle, phase, me_in[phase]] = row
        for off in range(1, GROUP):
            phase_copy(cycle, phase, off).start()

    def take_phase(cycle, phase):
        copy = phase_copy(cycle, phase, 1, GROUP - 1)
        copy.wait_recv()
        copy.wait_send()
        return jnp.sum(slots[cycle, phase], axis=0)

    def start_gram(cycle):
        def body(i, sums):
            sums = list(sums)
            for u in range(9):
                v = [basis[k, i * 9 + u] for k in range(5)]
                for a in range(5):
                    for b in range(a, 5):
                        e = pair_index(a, b)
                        sums[e] = sums[e] + v[a] * v[b]
            return tuple(sums)

        sums = lax.fori_loop(
            0, NODES // 9, body, tuple(jnp.zeros((8, ELEMS), F32) for _ in range(ENTRIES))
        )
        for e in range(ENTRIES):
            gacc[pl.ds(8 * e, 8), :] = sums[e]
        part = gacc[pl.ds(0, GROUP, stride=8), :]
        for r in range(1, 8):
            part = part + gacc[pl.ds(r, GROUP, stride=8), :]
        column = jnp.sum(part, axis=1, keepdims=True)
        row = jnp.sum(jnp.where(eye, column, 0.0), axis=0, keepdims=True)
        send_phase(cycle, 0, row)

    def middle_gram(cycle):
        send_phase(cycle, 1, take_phase(cycle, 0))

    def end_gram(cycle):
        row = take_phase(cycle, 1)
        spread = jnp.sum(jnp.where(eye, row, 0.0), axis=1, keepdims=True)
        spread = jnp.broadcast_to(spread, (GROUP, ELEMS))
        gram = [
            [spread[pair_index(i, j):pair_index(i, j) + 1] for j in range(5)] for i in range(5)
        ]
        half = [[gram[i][k] * thetas[k] + gram[i][k + 1] for k in range(4)] for i in range(5)]
        normal = [[half[j][k] * thetas[j] + half[j + 1][k] for k in range(4)] for j in range(4)]
        target = [gram[j][0] * thetas[j] + gram[j + 1][0] for j in range(4)]
        low = [[None] * 4 for _ in range(4)]
        scaled = [[None] * 4 for _ in range(4)]
        inverse = [None] * 4
        for j in range(4):
            for i in range(j, 4):
                value = normal[i][j]
                for m in range(j):
                    value = value - low[j][m] * scaled[i][m]
                scaled[i][j] = value
            inverse[j] = 1.0 / scaled[j][j]
            for i in range(j + 1, 4):
                low[i][j] = scaled[i][j] * inverse[j]
        fore = []
        for i in range(4):
            value = target[i]
            for m in range(i):
                value = value - low[i][m] * fore[m]
            fore.append(value)
        weights = [None] * 4
        for i in reversed(range(4)):
            value = fore[i] * inverse[i]
            for m in range(i + 1, 4):
                value = value - low[m][i] * weights[m]
            weights[i] = value
        combined = [weights[0] * thetas[0]]
        for i in range(1, 4):
            combined.append(weights[i] * thetas[i] + weights[i - 1])
        combined.append(weights[3])
        lanes = lax.broadcasted_iota(jnp.int32, (1, ELEMS), 1)
        line = jnp.zeros((1, ELEMS), F32)
        for i in range(4):
            line = jnp.where(lanes == i, weights[i], line)
        lines[pl.ds(cycle, 1), :] = line
        return weights, combined

    def next_cycle(cycle):
        weights, combined = end_gram(cycle)
        sets = [[1.0 - combined[0]] + [-value for value in combined[1:]]]
        for m in range(AHEAD):
            old = sets[-1]
            new = [None] * (len(old) + 1)
            for i, value in enumerate(old):
                here = value * (thetas[i % STEPS] - thetas[m])
                new[i] = here if new[i] is None else new[i] + here
                new[i + 1] = value
            sets.append(new)
        factor = jnp.broadcast_to(sets[AHEAD][-1], (8, ELEMS))
        masks[1] = masks[0] * factor
        weights8, combined8 = wide(weights), wide(combined)
        sets8 = [wide(one) for one in sets[1:]]

        def body(i, carry):
            for u in range(3):
                at = i * 3 + u
                v = [basis[k, at] for k in range(STEPS + AHEAD + 1)]
                total = adj[at]
                for k in range(STEPS):
                    total = total + weights8[k] * v[k]
                adj[at] = total
                fresh = v[0]
                for k in range(STEPS + 1):
                    fresh = fresh - combined8[k] * v[k]
                basis[0, at] = fresh
                for m in range(AHEAD):
                    total = sets8[m][0] * v[0]
                    for k in range(1, len(sets8[m])):
                        total = total + sets8[m][k] * v[k]
                    basis[m + 1, at] = total
            return carry

        lax.fori_loop(0, NODES // 3, body, 0)

    def last_cycle(cycle):
        weights, combined = end_gram(cycle)
        weights6, combined6 = wide(weights, NVAR), wide(combined, NVAR)
        for node in range(NODES):
            rows = pl.ds(node, NVAR, stride=NODES)
            v = [basis[k, node, vars6, :] for k in range(STEPS + 1)]
            total = adj[node, vars6, :]
            for k in range(STEPS):
                total = total + weights6[k] * v[k]
            done[0, rows, :] = total
            fresh = v[0]
            for k in range(STEPS + 1):
                fresh = fresh - combined6[k] * v[k]
            done[1, rows, :] = fresh

        adj_out[...] = done[0, pl.ds(0, BLOCK), :]
        res_out[...] = done[1, pl.ds(0, BLOCK), :]
        coef_out[...] = lines[pl.ds(0, CYCLES), :][:, :STEPS]

    def product(step, k, theta, first):
        for slot, one in ((0, middle), (1, far), (None, outer), (None, near)):
            if first:
                face_copy(*one).wait()
            send_face(step, k, *one, first, slot)
        to = k + 1
        if not first:
            sent(step - 1)
            place = lax.rem(step, 4)
            cycle = step // 4 - 1

            @pl.when(jnp.logical_and(place == 0, step >= STEPS))
            def _():
                start_gram(cycle)

        else:
            face_copy(2, 0).wait()
            face_copy(2, 1).wait()
        local_faces(k, first)
        diag_product(k, first)
        own_part(k, theta)
        masks[1] = masks[0]
        if not first:

            @pl.when(jnp.logical_and(place == 1, step >= STEPS))
            def _():
                middle_gram(cycle)

            @pl.when(jnp.logical_and(place == 3, step >= STEPS))
            def _():
                next_cycle(cycle)

            to = jnp.where(k == STEPS + AHEAD - 1, AHEAD, to)
        for one in (near, outer, far, middle):
            arrive(step, to, *one)

    product(0, 0, thetas[0], True)

    def step_body(step, carry):
        k = jnp.where(step < STEPS, step, lax.rem(step, STEPS) + STEPS)
        product(step, k, shifts[order[lax.rem(k, STEPS)]], False)
        return carry

    lax.fori_loop(1, TOTAL, step_body, 0)
    start_gram(CYCLES - 1)
    sent(TOTAL - 1)
    middle_gram(CYCLES - 1)
    last_cycle(CYCLES - 1)


def wide(values, rows=8):
    return [jnp.broadcast_to(value, (rows, ELEMS)) for value in values]


def copy_kernel(a, b, c, x, y, z):
    x[...] = a[...]
    y[...] = b[...]
    z[...] = c[...]


def hand_out(arrays):
    vmem = pl.BlockSpec(memory_space=pltpu.VMEM)
    return pl.pallas_call(
        copy_kernel,
        out_shape=tuple(jax.ShapeDtypeStruct(one.shape, one.dtype) for one in arrays),
        in_specs=[vmem] * 3,
        out_specs=(vmem,) * 3,
    )(*arrays)


def on_device(right_side, diag_blocks, face_blocks, orient_codes, live_counts, shifts, shift_order):
    vmem = pl.BlockSpec(memory_space=pltpu.VMEM)
    hbm = pl.BlockSpec(memory_space=pltpu.HBM)
    arrays = pl.pallas_call(
        kernel,
        out_shape=(
            jax.ShapeDtypeStruct((BLOCK, ELEMS), F32),
            jax.ShapeDtypeStruct((BLOCK, ELEMS), F32),
            jax.ShapeDtypeStruct((CYCLES, STEPS), F32),
        ),
        in_specs=[hbm] * 7,
        out_specs=(vmem, vmem, vmem),
        scratch_shapes=[
            pltpu.VMEM((BLOCK, BLOCK, ELEMS), jnp.bfloat16),
            pltpu.VMEM((6, FACE, FACE, ELEMS), jnp.bfloat16),
            pltpu.VMEM((2, FACE, FACE, ELEMS), F32),
            pltpu.VMEM((WIDE, ELEMS), F32),
            pltpu.VMEM((16, ELEMS), jnp.int32),
            pltpu.SMEM((1,), jnp.int32),
            pltpu.SMEM((STEPS,), F32),
            pltpu.SMEM((STEPS,), jnp.int32),
            pltpu.VMEM((STEPS + AHEAD + 1, NODES, 8, ELEMS), F32),
            pltpu.VMEM((NODES, 8, ELEMS), F32),
            pltpu.VMEM((6, 72, ELEMS), F32),
            pltpu.VMEM((WIDE, ELEMS), F32),
            pltpu.VMEM((2, 9, NVAR, ELEMS), F32),
            pltpu.VMEM((2, 8, ELEMS), F32),
            pltpu.VMEM((TOTAL, 4, 9, NVAR, ELEMS), F32),
            pltpu.VMEM((TOTAL, 4, 9, NVAR, ELEMS), F32),
            pltpu.VMEM((GROUP * 8, ELEMS), F32),
            pltpu.VMEM((CYCLES + 1, 2, GROUP, 1, ELEMS), F32),
            pltpu.VMEM((16, ELEMS), F32),
            pltpu.VMEM((2, WIDE, ELEMS), F32),
            pltpu.SemaphoreType.DMA((5,)),
            pltpu.SemaphoreType.DMA((BLOCK // CHUNK,)),
            pltpu.SemaphoreType.DMA((6,)),
            pltpu.SemaphoreType.DMA((TOTAL, 4)),
            pltpu.SemaphoreType.DMA((TOTAL, 4)),
            pltpu.SemaphoreType.DMA((CYCLES, 2)),
            pltpu.SemaphoreType.DMA((CYCLES, 2)),
        ],
        compiler_params=pltpu.CompilerParams(
            collective_id=0, has_side_effects=True, vmem_limit_bytes=56 * 2**20
        ),
    )(right_side, diag_blocks, face_blocks, orient_codes, live_counts, shifts, shift_order)
    return hand_out(arrays)


def solution(mesh):
    placed = (
        P(None, ("span", "chord")),
        P(None, None, ("span", "chord")),
        P(None, None, None, ("span", "chord")),
        P(None, ("span", "chord")),
        P(("span", "chord")),
        P(),
        P(),
    )
    return jax.shard_map(
        on_device,
        mesh=mesh,
        in_specs=placed,
        out_specs=(P(None, ("span", "chord")), P(None, ("span", "chord")), P()),
        check_vma=False,
    )
```
